512 devices in a mesh: row: 16 (over x, y_hi, core), col: 32 (over y_lo, z).
Axes of the slice: x: 4, y: 8 (y_hi: 2, y_lo: 4; y = y_hi * 4 + y_lo), z: 8, core: 2. Of those that a mesh axis runs over, the one named last changes fastest.
Arguments:
- orbitals: bfloat16 [8192, 8192], P(('row', 'col')), may hold values from -0.0625 to 0.0625
- targets: bfloat16 [8192, 1024], P(('row', 'col')), may hold values from -6 to 6
- coulomb: float32 [8192, 8192], P('row', 'col'), as said below
Outputs:
- applied: float32 [8192, 1024], P(('row', 'col'))
The draws below stay inside these ranges and needn't reach their ends.
Inputs may be any that keep to these rules, and one draw needn't show every extreme that they name: `coulomb`: the Coulomb matrix V over points defined in the reference program is symmetric: V[p, s] = V[s, p] exactly.
All inputs are finite; a program needn't handle non-finite values.
Results may differ from the reference program's by a relative error of at most 0.005.
Values may be sent and summed in bfloat16 or wider, within the bound.
A program may use at most 64 MiB of HBM per device.

```python
import jax
import jax.numpy as jnp
from jax import lax

PTS_DEV = 16
NOCC = 8192
NB = 1024
NP = 8192
N_ROW = 16
N_COL = 32


def draw_coulomb(key, part):
    key = jax.random.fold_in(key, 5)
    total = PTS_DEV * N_ROW * N_COL
    key_pos, key_noise = jax.random.split(key)
    places = jax.random.uniform(key_pos, (total, 3), jnp.float32) * 4.0
    dist = jnp.zeros((total, total), jnp.float32)
    for axis_id in range(3):
        coord = places[:, axis_id]
        dist = dist + (coord[:, None] - coord[None, :]) ** 2
    smooth = 1.0 / (1.0 + dist)
    noise = jax.random.normal(key_noise, (total, total), jnp.float32)
    weight_smooth = 2.0
    sym = (noise + noise.T) * 0.70710678
    full = (weight_smooth * smooth + sym) / jnp.sqrt(jnp.float32(total))
    return full.reshape(total, N_ROW, N_COL, PTS_DEV).transpose(0, 2, 1, 3).reshape(total, total)


def steps_of(own_key, shape, cuts, low, high):
    def one(dim, shards_of):
        heights = jax.random.uniform(jax.random.fold_in(jax.random.fold_in(own_key, 6), dim), (shards_of,), jnp.float32, low / len(cuts), high / len(cuts))
        return jnp.repeat(jnp.exp(heights), shape[dim] // shards_of).reshape((-1,) + (1,) * (len(shape) - dim - 1))

    gain = one(*cuts[0])
    for cut in cuts[1:]:
        gain = gain * one(*cut)
    return gain


def centred(stream_key, extent, deviation, reach, shards=(), kind=jnp.bfloat16):
    gain = steps_of(stream_key, extent, shards, -0.22, 0.18) if shards else 1.0
    entries = jax.random.normal(stream_key, extent, jnp.float32) * deviation * gain
    return jnp.minimum(jnp.maximum(entries, -reach), reach).astype(kind)


def setup_inputs(seed: int = 0) -> dict:
    arg_keys = jax.random.split(jax.random.key(seed), 4)
    return {
        "orbitals": centred(arg_keys[0], (NP, NOCC), NOCC ** -0.5, 0.0625, ((0, 512),)),
        "targets": centred(arg_keys[1], (NP, NB), 1.0, 6.0, ((0, 512),)),
        "coulomb": draw_coulomb(jax.random.fold_in(arg_keys[3], 71), 0),
    }


def reference(orbitals, targets, coulomb):
    total = orbitals.shape[0]
    potential = coulomb.reshape(total, N_COL, N_ROW, PTS_DEV).transpose(0, 2, 1, 3).reshape(total, total)
    pairs = lax.dot_general(orbitals, orbitals, (((1,), (1,)), ((), ())), preferred_element_type=jnp.float32)
    screened = (pairs * potential).astype(jnp.bfloat16)
    return jnp.dot(screened, targets, preferred_element_type=jnp.float32)
```

```python
import functools

import jax
import jax.numpy as jnp
from jax import lax
from jax.experimental import pallas as pl
from jax.experimental.pallas import tpu as pltpu
from jax.sharding import PartitionSpec as P

MESH = pl.DeviceIdType.MESH
F32 = jnp.float32
BF16 = jnp.bfloat16
KS = 1024
NB = 1024

SLOT = {4: 0, 0: 1, 1: 2, -1: 3, 2: 4, -2: 5, 3: 6, -3: 7, -4: 0}
OFFSET = (4, 0, 1, -1, 2, -2, 3, -3)
RECTS = ((1, 6, 1, 6), (6, 8, 1, 8), (1, 6, 6, 8), (0, 1, 0, 8), (1, 8, 0, 1))
DX = (0, 1, 3, 2)


def kernel(
    orb, tgt, cou, out,
    A, B, T, SB, RB, OWN, XS, XR, VF, VB, VR, S, OB, OR, OO,
    loc, a_s, a_r, g_s, g_r, t_s, t_r, v_s, v_r, d_s, d_r, x_s, x_r, o_s, o_r,
):
    row, col = lax.axis_index("row"), lax.axis_index("col")
    x, yh, c = lax.div(row, 4), lax.rem(lax.div(row, 2), 2), lax.rem(row, 2)
    yl, z = lax.div(col, 8), lax.rem(col, 8)
    y = yh * 4 + yl
    sib = 1 - c

    def dev(x_, y_, z_, c_):
        return ((x_ * 2 + lax.div(y_, 4)) * 2 + c_, lax.rem(y_, 4) * 8 + z_)

    def at(dx=0, dy=0, dz=0, dc=0):
        return dev(
            lax.rem(x + dx + 4, 4), lax.rem(y + dy + 8, 8), lax.rem(z + dz + 8, 8), sib if dc else c
        )

    def yl_peer(d):
        return (row, lax.rem(yl + d, 4) * 8 + z)

    started = []

    def remote(src, dst, ss, rs, to):
        return pltpu.make_async_remote_copy(
            src_ref=src, dst_ref=dst, send_sem=ss, recv_sem=rs, device_id=to, device_id_type=MESH
        )

    def go(cp):
        cp.start()
        started.append(cp)
        return cp

    own_slice = lambda g: orb.at[:, pl.ds(pl.multiple_of(g * KS, KS), KS)]

    v_in = pltpu.make_async_copy(cou, VF, loc.at[0])
    v_in.start()
    t_in = pltpu.make_async_copy(tgt, T.at[1, x, c], loc.at[1])
    t_in.start()
    a_in = pltpu.make_async_copy(own_slice(x * 2 + c), A.at[1, x, c], loc.at[2])
    a_in.start()

    barrier = pltpu.get_barrier_semaphore()
    partners = [at(dx=dx, dc=dc) for dx in range(4) for dc in range(2) if dx or dc]
    partners += [at(dy=1), at(dy=-1)] + [at(dz=d) for d in range(1, 8)] + [yl_peer(d) for d in (1, 2, 3)]
    for p in partners:
        pl.semaphore_signal(barrier, inc=1, device_id=p, device_id_type=MESH)
    pl.semaphore_wait(barrier, len(partners))

    swaps = {}
    for i, dx in enumerate(DX):
        for dc in (1, 0):
            if dx or dc:
                n = dx * 2 + dc - 1
                xp = lax.rem(x + dx, 4)
                cp_ = sib if dc else c
                swaps[dx, dc] = go(
                    remote(own_slice(xp * 2 + cp_), A.at[1, x, c], a_s.at[n], a_r.at[n], at(dx=dx, dc=dc))
                )

    def t_ring(d, s):
        sg = -1 if d == 0 else 1
        src = tgt if s == 1 else T.at[SLOT[sg * (s - 1)], x, c]
        n = d * 4 + s - 1
        return remote(src, T.at[SLOT[sg * s], x, c], t_s.at[n], t_r.at[n], at(dy=-sg))

    tr = {(d, 1): go(t_ring(d, 1)) for d in (0, 1)}

    chunk = [lax.rem(x - dx + 4, 4) for dx in DX]

    def ring(kind, d, s, i):
        sg = -1 if d == 0 else 1
        buf = B if kind else A
        src = A if s == 1 else buf
        n = ((kind * 2 + d) * 4 + s - 1) * 4 + i
        to = at(dy=-sg) if kind else at(dz=-sg)
        return remote(
            src.at[SLOT[sg * (s - 1)], chunk[i]], buf.at[SLOT[sg * s], chunk[i]], g_s.at[n], g_r.at[n], to
        )

    rg = {}

    def forward(s, i):
        for kind in (1, 0):
            for d in (0, 1):
                if s > 1:
                    rg[kind, d, s - 1, i].wait_recv()
                if s < 4 or (d == 0) == (i < 2):
                    rg[kind, d, s, i] = go(ring(kind, d, s, i))

    b_own = []
    for i, dx in enumerate(DX):
        if dx == 0:
            a_in.wait()
            swaps[0, 1].wait_recv()
        else:
            swaps[dx, 0].wait_recv()
            swaps[dx, 1].wait_recv()
        forward(1, i)
        cp = pltpu.make_async_copy(A.at[1, chunk[i]], B.at[1, chunk[i]], loc.at[3 + i])
        cp.start()
        b_own.append(cp)

    def t_forward(s):
        for d in (0, 1):
            if (d, s - 1) in tr:
                tr[d, s - 1].wait_recv()
            if s < 4 or d == 0:
                if s < 5:
                    tr[d, s] = go(t_ring(d, s))

    t_forward(2)

    v_in.wait()
    dst = lax.broadcasted_iota(jnp.int32, (256, 256), 1)
    src = lax.broadcasted_iota(jnp.int32, (256, 256), 0)
    want = ((dst & 127) >> 5) * 64 + (dst >> 7) * 32 + (dst & 31)
    perm = jnp.where(src == want, 1.0, 0.0).astype(BF16)
    for q in range(4):
        moved = jnp.dot(VF[q * 128:(q + 1) * 128, :].astype(BF16), perm, preferred_element_type=F32).astype(BF16)
        VB[q, 0] = moved[:, :128].reshape(8, 16, 128)
        VB[q, 1] = moved[:, 128:].reshape(8, 16, 128)
    v_own = pltpu.make_async_copy(VB.at[yl], VR.at[yl], loc.at[7])
    v_own.start()

    dd, xx = {}, {}

    def compute(n):
        r0, r1, c0, c1 = RECTS[n]
        rows = (r1 - r0) * 64
        for half in (0, 1):
            left = A[r0:r1, :, c if half else sib].reshape(rows, KS)
            q = c0
            while q < c1:
                w = min(2 - (q & 1), c1 - q)
                right = B[q:q + w].reshape(w * 128, KS)
                tile = lax.dot_general(left, right, (((1,), (1,)), ((), ())), preferred_element_type=F32)
                tile = tile.reshape(r1 - r0, 4, 16, w * 128)
                if half:
                    OWN[r0:r1, :, :, q * 128:(q + w) * 128] = tile
                else:
                    SB[r0:r1, :, :, q * 128:(q + w) * 128] = tile.astype(BF16)
                q += w
            if not half:
                where = (slice(r0, r1), slice(None), slice(None), slice(c0 * 128, c1 * 128))
                dd[n] = go(remote(SB.at[where], RB.at[where], d_s.at[n], d_r.at[n], at(dc=1)))

    def combine(n):
        r0, r1, c0, c1 = RECTS[n]
        cols = slice(c0 * 128, c1 * 128)
        dd[n].wait_recv()
        for dx in (2, 1, 3):
            xp = lax.rem(x + dx, 4)
            for r in range(r0, r1):
                XS[dx - 1, r, :, cols] = (OWN[r, xp, :, cols] + RB[r, xp, :, cols].astype(F32)).astype(BF16)
            k = n * 3 + dx - 1
            where = (dx - 1, slice(r0, r1), slice(None), cols)
            xx[n, dx] = go(remote(XS.at[where], XR.at[where], x_s.at[k], x_r.at[k], at(dx=dx)))

    def finish(n):
        r0, r1, c0, c1 = RECTS[n]
        for dx in (1, 2, 3):
            xx[n, dx].wait_recv()
        for q in range(c0, c1):
            yq = lax.rem(y + OFFSET[q] + 8, 8)
            cols = slice(q * 128, (q + 1) * 128)
            for r in range(r0, r1):
                zr = lax.rem(z + OFFSET[r] + 8, 8)
                pairs = OWN[r, x, :, cols] + RB[r, x, :, cols].astype(F32)
                for k in range(3):
                    pairs = pairs + XR[k, r, :, cols].astype(F32)
                v = VR[lax.rem(yq, 4), lax.div(yq, 4), zr].astype(F32)
                S[r, :, cols] = (pairs * v).astype(BF16)

    xm, xp1, xf = lax.rem(x + 3, 4), lax.rem(x + 1, 4), lax.rem(x + 2, 4)
    tx, td = {}, {}

    def t_sib(k, xv):
        td[k] = go(remote(T.at[:, xv, c], T.at[:, xv, c], t_s.at[12 + k], t_r.at[12 + k], at(dc=1)))

    def t_first():
        tx[0] = go(remote(T.at[:, x, c], T.at[:, x, c], t_s.at[8], t_r.at[8], at(dx=1)))
        tx[1] = go(remote(T.at[:, x, c], T.at[:, x, c], t_s.at[9], t_r.at[9], at(dx=-1)))
        t_sib(0, x)

    def t_second():
        tx[0].wait_recv()
        tx[2] = go(remote(T.at[0:4, xm, c], T.at[0:4, xm, c], t_s.at[10], t_r.at[10], at(dx=1)))
        tx[1].wait_recv()
        tx[3] = go(remote(T.at[4:8, xp1, c], T.at[4:8, xp1, c], t_s.at[11], t_r.at[11], at(dx=-1)))
        t_sib(1, xm)
        t_sib(2, xp1)

    def t_third():
        tx[2].wait_recv()
        tx[3].wait_recv()
        t_sib(3, xf)

    for i in range(4):
        forward(2, i)
        if i == 0:
            t_forward(3)
        if i == 2:
            t_forward(4)
    t_forward(5)
    t_in.wait()
    t_first()
    for i in range(4):
        forward(3, i)
    for cp in b_own:
        cp.wait()
    compute(0)
    for i in range(4):
        forward(4, i)
        if i == 1:
            combine(0)
    t_second()
    v_out = []
    for d in (1, 2, 3):
        v_out.append(
            go(remote(VB.at[lax.rem(yl + d, 4)], VR.at[yl], v_s.at[d - 1], v_r.at[d - 1], yl_peer(d)))
        )
    compute(1)
    compute(2)
    combine(1)
    combine(2)
    t_third()
    for i in range(4):
        for kind in (1, 0):
            rg[kind, 0 if i < 2 else 1, 4, i].wait_recv()
    compute(3)
    compute(4)
    combine(3)
    combine(4)
    v_own.wait()
    for cp in v_out:
        cp.wait_recv()
    for n in range(5):
        finish(n)
    for k in range(4):
        td[k].wait_recv()

    left = S[...].reshape(128, 1024)
    for q in range(4):
        cols = slice(q * 256, (q + 1) * 256)
        part = jnp.dot(left, T[:, :, :, :, cols].reshape(1024, 256), preferred_element_type=F32)
        part = part.reshape(8, 16, 256)
        OO[:, cols] = part[1]
        OB[:, :, cols] = part.astype(BF16)
    oo = []
    for o in (4, 3, -3, 2, -2, 1, -1):
        s = SLOT[o]
        n = s if s == 0 else s - 1
        oo.append(go(remote(OB.at[s], OR.at[n], o_s.at[n], o_r.at[n], at(dz=o))))
    for cp in oo:
        cp.wait_recv()
    total = OO[...]
    for n in range(7):
        total = total + OR[n].astype(F32)
    out[...] = total
    for cp in started:
        cp.wait_send()


def body(orbitals, targets, coulomb):
    any_, dma = pl.BlockSpec(memory_space=pl.ANY), pltpu.SemaphoreType.DMA
    return pl.pallas_call(
        kernel,
        out_shape=jax.ShapeDtypeStruct((16, NB), F32),
        in_specs=[any_] * 3,
        out_specs=pl.BlockSpec(memory_space=pltpu.VMEM),
        scratch_shapes=[
            pltpu.VMEM((8, 4, 2, 16, KS), BF16),
            pltpu.VMEM((8, 4, 2, 16, KS), BF16),
            pltpu.VMEM((8, 4, 2, 16, NB), BF16),
            pltpu.VMEM((8, 4, 16, 1024), BF16),
            pltpu.VMEM((8, 4, 16, 1024), BF16),
            pltpu.VMEM((8, 4, 16, 1024), F32),
            pltpu.VMEM((3, 8, 16, 1024), BF16),
            pltpu.VMEM((3, 8, 16, 1024), BF16),
            pltpu.VMEM((512, 256), F32),
            pltpu.VMEM((4, 2, 8, 16, 128), BF16),
            pltpu.VMEM((4, 2, 8, 16, 128), BF16),
            pltpu.VMEM((8, 16, 1024), BF16),
            pltpu.VMEM((8, 16, NB), BF16),
            pltpu.VMEM((7, 16, NB), BF16),
            pltpu.VMEM((16, NB), F32),
            dma((8,)),
            dma((7,)), dma((7,)),
            dma((64,)), dma((64,)),
            dma((16,)), dma((16,)),
            dma((3,)), dma((3,)),
            dma((5,)), dma((5,)),
            dma((15,)), dma((15,)),
            dma((7,)), dma((7,)),
        ],
        compiler_params=pltpu.CompilerParams(
            collective_id=0, has_side_effects=True, vmem_limit_bytes=40 * 1024 * 1024
        ),
        cost_estimate=pl.CostEstimate(flops=2_500_000_000, bytes_accessed=4_000_000, transcendentals=0),
    )(orbitals, targets, coulomb)


def solution(mesh):
    in_specs = (P(("row", "col"), None), P(("row", "col"), None), P("row", "col"))
    return jax.shard_map(
        body, mesh=mesh, in_specs=in_specs, out_specs=P(("row", "col"), None), check_vma=False
    )
```

```python
import functools

import jax
import jax.numpy as jnp
from jax import lax
from jax.experimental import pallas as pl
from jax.experimental.pallas import tpu as pltpu
from jax.sharding import PartitionSpec as P

MESH = pl.DeviceIdType.MESH
F32 = jnp.float32
BF16 = jnp.bfloat16
KS = 1024
NB = 1024

SLOT = {4: 0, 0: 1, 1: 2, -1: 3, 2: 4, -2: 5, 3: 6, -3: 7, -4: 0}
OFFSET = (4, 0, 1, -1, 2, -2, 3, -3)
RECTS = ((1, 6, 1, 6), (6, 8, 1, 8), (1, 6, 6, 8), (0, 1, 1, 8), (0, 8, 0, 1))
HALVES = (
    ((slice(1, 4), slice(128, 768)), (slice(4, 6), slice(128, 768))),
    ((slice(6, 7), slice(128, 1024)), (slice(7, 8), slice(128, 1024))),
    ((slice(1, 6), slice(768, 896)), (slice(1, 6), slice(896, 1024))),
)
DX = (0, 1, 3, 2)


def kernel(
    orb, tgt, cou, out,
    W, A, B, T, SB, RB, OWN, XS, XR, YS, YR, VF, VB, VR, S, OB, OA, OH, OC, OR, OO,
    loc, a_s, a_r, g_s, g_r, t_s, t_r, v_s, v_r, d_s, d_r, x_s, x_r, o_s, o_r,
):
    row, col = lax.axis_index("row"), lax.axis_index("col")
    x, yh, c = lax.div(row, 4), lax.rem(lax.div(row, 2), 2), lax.rem(row, 2)
    yl, z = lax.div(col, 8), lax.rem(col, 8)
    y = yh * 4 + yl
    sib = 1 - c

    def dev(x_, y_, z_, c_):
        return ((x_ * 2 + lax.div(y_, 4)) * 2 + c_, lax.rem(y_, 4) * 8 + z_)

    def at(dx=0, dy=0, dz=0, dc=0):
        return dev(
            lax.rem(x + dx + 4, 4), lax.rem(y + dy + 8, 8), lax.rem(z + dz + 8, 8), sib if dc else c
        )

    def yl_peer(d):
        return (row, lax.rem(yl + d, 4) * 8 + z)

    started = []
    tr = {}

    def remote(src, dst, ss, rs, to):
        return pltpu.make_async_remote_copy(
            src_ref=src, dst_ref=dst, send_sem=ss, recv_sem=rs, device_id=to, device_id_type=MESH
        )

    def go(cp):
        cp.start()
        started.append(cp)
        return cp

    def own_slice(ref, g):
        return ref.at[:, pl.ds(pl.multiple_of(g * KS, KS), KS)]

    w_in = pltpu.make_async_copy(orb, W, loc.at[8])
    w_in.start()
    v_in = pltpu.make_async_copy(cou, VF, loc.at[0])
    v_in.start()
    t_in = pltpu.make_async_copy(tgt, T.at[1, x, c], loc.at[1])
    t_in.start()
    a_in = pltpu.make_async_copy(own_slice(orb, x * 2 + c), A.at[1, x, c], loc.at[2])
    a_in.start()

    barrier = pltpu.get_barrier_semaphore()
    partners = [at(dx=dx, dc=dc) for dx in range(4) for dc in range(2) if dx or dc]
    partners += [at(dy=d) for d in (1, -1, 2, -2)] + [at(dz=d) for d in (1, -1, 2, -2)] + [yl_peer(d) for d in (1, 2, 3)]
    for p in partners:
        pl.semaphore_signal(barrier, inc=1, device_id=p, device_id_type=MESH)
    pl.semaphore_wait(barrier, len(partners))

    def t_send(n, d, src, dst, cols, far):
        cp = remote(
            T.at[SLOT[src], x, c, :, cols], T.at[SLOT[dst], x, c, :, cols], t_s.at[n], t_r.at[n],
            at(dy=far * (1 - 2 * d)),
        )
        tr[n] = go(cp)

    whole, half = slice(0, NB), (slice(0, NB // 2), slice(NB // 2, NB))

    def t_start():
        for d in (0, 1):
            sg = 2 * d - 1
            t_send(d, d, 0, 2 * sg, whole, 2)
            t_send(2 + d, d, 0, sg, whole, 1)

    def t_on():
        for d in (0, 1):
            sg = 2 * d - 1
            tr[d].wait_recv()
            t_send(4 + d, d, 2 * sg, 3 * sg, whole, 1)
            t_send(6 + d, d, 2 * sg, 4 * sg, half[d], 2)

    swaps = {}
    w_in.wait()
    t_in.wait()
    for i, dx in enumerate(DX):
        for dc in (1, 0):
            if dx or dc:
                n = dx * 2 + dc - 1
                xp = lax.rem(x + dx, 4)
                cp_ = sib if dc else c
                swaps[dx, dc] = go(
                    remote(own_slice(W, xp * 2 + cp_), A.at[1, x, c], a_s.at[n], a_r.at[n], at(dx=dx, dc=dc))
                )

    t_start()

    chunk = [lax.rem(x - dx + 4, 4) for dx in DX]

    def ring(kind, d, s, i):
        sg = -1 if d == 0 else 1
        buf = B if kind else A
        src = A if s == 1 else buf
        n = ((kind * 2 + d) * 4 + s - 1) * 4 + i
        to = at(dy=-sg) if kind else at(dz=-sg)
        return remote(
            src.at[SLOT[sg * (s - 1)], chunk[i]], buf.at[SLOT[sg * s], chunk[i]], g_s.at[n], g_r.at[n], to
        )

    rg = {}

    def forward(s, i):
        for kind in (1, 0):
            for d in (0, 1):
                if s > 1:
                    rg[kind, d, s - 1, i].wait_recv()
                if s < 4 or (d == 0) == (i < 2):
                    rg[kind, d, s, i] = go(ring(kind, d, s, i))

    b_own = []
    for i, dx in enumerate(DX):
        if dx == 0:
            a_in.wait()
            swaps[0, 1].wait_recv()
        else:
            swaps[dx, 0].wait_recv()
            swaps[dx, 1].wait_recv()
        forward(1, i)
        cp = pltpu.make_async_copy(A.at[1, chunk[i]], B.at[1, chunk[i]], loc.at[3 + i])
        cp.start()
        b_own.append(cp)
    t_on()

    v_in.wait()
    dst = lax.broadcasted_iota(jnp.int32, (256, 256), 1)
    src = lax.broadcasted_iota(jnp.int32, (256, 256), 0)
    want = ((dst & 127) >> 5) * 64 + (dst >> 7) * 32 + (dst & 31)
    perm = jnp.where(src == want, 1.0, 0.0).astype(BF16)
    for q in range(4):
        moved = jnp.dot(VF[q * 128:(q + 1) * 128, :].astype(BF16), perm, preferred_element_type=F32).astype(BF16)
        VB[q, 0] = moved[:, :128].reshape(8, 16, 128)
        VB[q, 1] = moved[:, 128:].reshape(8, 16, 128)
    v_own = pltpu.make_async_copy(VB.at[yl], VR.at[yl], loc.at[7])
    v_own.start()

    dd, xx = {}, {}

    def compute(n):
        r0, r1, c0, c1 = RECTS[n]
        rows = (r1 - r0) * 64
        left = jnp.concatenate(
            [A[r0:r1, :, sib].reshape(rows, KS), A[r0:r1, :, c].reshape(rows, KS)], axis=0
        )
        q = c0
        while q < c1:
            w = min(2 - (q & 1), c1 - q)
            right = B[q:q + w].reshape(w * 128, KS)
            tile = lax.dot_general(left, right, (((1,), (1,)), ((), ())), preferred_element_type=F32)
            tile = tile.reshape(2, r1 - r0, 4, 16, w * 128)
            cols = slice(q * 128, (q + w) * 128)
            SB[r0:r1, :, :, cols] = tile[0].astype(BF16)
            OWN[r0:r1, :, :, cols] = tile[1]
            q += w
        where = (slice(r0, r1), slice(None), slice(None), slice(c0 * 128, c1 * 128))
        dd[n] = go(remote(SB.at[where], RB.at[where], d_s.at[n], d_r.at[n], at(dc=1)))

    xm, xp1, xf = lax.rem(x + 3, 4), lax.rem(x + 1, 4), lax.rem(x + 2, 4)

    def x_send(n, k, src, dst, d, rows, cols):
        where = (d, rows, slice(None), cols)
        xx[n, k, d] = go(
            remote(src.at[where], dst.at[where], x_s.at[n * 4 + k * 2 + d], x_r.at[n * 4 + k * 2 + d], at(dx=1 - 2 * d))
        )

    def spread(n):
        dd[n].wait_recv()
        for d in (0, 1):
            rows, cols = HALVES[n][d]
            for r in range(rows.start, rows.stop):
                XS[d, r, :, cols] = (OWN[r, xf, :, cols] + RB[r, xf, :, cols].astype(F32)).astype(BF16)
            x_send(n, 0, XS, XR, d, rows, cols)

    def combine(n):
        r0, r1, c0, c1 = RECTS[n]
        for d in (0, 1):
            xx[n, 0, d].wait_recv()
            to = xm if d else xp1
            for h in (0, 1):
                rows, cols = HALVES[n][h]
                for r in range(rows.start, rows.stop):
                    part = OWN[r, to, :, cols] + RB[r, to, :, cols].astype(F32)
                    if h == d:
                        part = part + XR[d, r, :, cols].astype(F32)
                    YS[d, r, :, cols] = part.astype(BF16)
            x_send(n, 1, YS, YR, d, slice(r0, r1), slice(c0 * 128, c1 * 128))

    def direct(n):
        r0, r1, c0, c1 = RECTS[n]
        rows, cols = slice(r0, r1), slice(c0 * 128, c1 * 128)
        dd[n].wait_recv()
        for k, buf, land, to, dx in ((2, XS, XR, xf, 2), (0, YS, YR, xp1, 1), (1, YS, YR, xm, -1)):
            j = k % 2
            for r in range(r0, r1):
                buf[j, r, :, cols] = (OWN[r, to, :, cols] + RB[r, to, :, cols].astype(F32)).astype(BF16)
            where = (j, rows, slice(None), cols)
            m = n * 4 + k
            xx[n, 1, k] = go(remote(buf.at[where], land.at[where], x_s.at[m], x_r.at[m], at(dx=dx)))

    def finish(n):
        r0, r1, c0, c1 = RECTS[n]
        for d in (0, 1, 2):
            if (n, 1, d) in xx:
                xx[n, 1, d].wait_recv()
        for q in range(c0, c1):
            yq = lax.rem(y + OFFSET[q] + 8, 8)
            cols = slice(q * 128, (q + 1) * 128)
            for r in range(r0, r1):
                zr = lax.rem(z + OFFSET[r] + 8, 8)
                pairs = OWN[r, x, :, cols] + RB[r, x, :, cols].astype(F32)
                for d in (0, 1):
                    pairs = pairs + YR[d, r, :, cols].astype(F32)
                if n > 2:
                    pairs = pairs + XR[0, r, :, cols].astype(F32)
                v = VR[lax.rem(yq, 4), lax.div(yq, 4), zr].astype(F32)
                S[r, :, cols] = (pairs * v).astype(BF16)

    tx, td = {}, {}

    def t_sib(k, xv):
        td[k] = go(remote(T.at[:, xv, c], T.at[:, xv, c], t_s.at[12 + k], t_r.at[12 + k], at(dc=1)))

    def t_first():
        for n in range(2, 8):
            tr[n].wait_recv()
        tx[0] = go(remote(T.at[:, x, c], T.at[:, x, c], t_s.at[8], t_r.at[8], at(dx=1)))
        tx[1] = go(remote(T.at[:, x, c], T.at[:, x, c], t_s.at[9], t_r.at[9], at(dx=-1)))
        t_sib(0, x)

    def t_second():
        tx[0].wait_recv()
        tx[2] = go(remote(T.at[0:4, xm, c], T.at[0:4, xm, c], t_s.at[10], t_r.at[10], at(dx=1)))
        tx[1].wait_recv()
        tx[3] = go(remote(T.at[4:8, xp1, c], T.at[4:8, xp1, c], t_s.at[11], t_r.at[11], at(dx=-1)))
        t_sib(1, xm)
        t_sib(2, xp1)

    def t_third():
        tx[2].wait_recv()
        tx[3].wait_recv()
        t_sib(3, xf)

    for i in range(4):
        forward(2, i)
    t_first()
    for i in range(4):
        forward(3, i)
    for cp in b_own:
        cp.wait()
    compute(0)
    for i in range(4):
        forward(4, i)
        if i == 0:
            spread(0)
            t_second()
    compute(1)
    compute(2)
    combine(0)
    spread(1)
    spread(2)
    for i in range(4):
        rg[0, i // 2, 4, i].wait_recv()
    compute(3)
    for i in range(4):
        rg[1, i // 2, 4, i].wait_recv()
    v_out = []
    for d in (1, 2, 3):
        v_out.append(
            go(remote(VB.at[lax.rem(yl + d, 4)], VR.at[yl], v_s.at[d - 1], v_r.at[d - 1], yl_peer(d)))
        )
    compute(4)
    direct(3)
    direct(4)
    combine(1)
    combine(2)
    t_third()
    v_own.wait()
    for cp in v_out:
        cp.wait_recv()
    for n in range(5):
        finish(n)
    for k in range(4):
        td[k].wait_recv()

    left = S[...].reshape(128, 1024)
    for q in range(4):
        cols = slice(q * 256, (q + 1) * 256)
        part = jnp.dot(left, T[:, :, :, :, cols].reshape(1024, 256), preferred_element_type=F32)
        part = part.reshape(8, 16, 256)
        for k in range(3):
            OO[k, :, cols] = part[SLOT[(0, 2, -2)[k]]]
        OB[:, :, cols] = part.astype(BF16)

    def o_send(n, src, dst, dz):
        return go(remote(src, dst, o_s.at[n], o_r.at[n], at(dz=dz)))

    far = [o_send(d, OB.at[0, :, half[d]], OH.at[d], 2 - 4 * d) for d in (0, 1)]
    far += [o_send(2 + d, OB.at[SLOT[3 - 6 * d]], OA.at[d], 1 - 2 * d) for d in (0, 1)]
    near = [o_send(4 + d, OB.at[SLOT[1 - 2 * d]], OR.at[d], 1 - 2 * d) for d in (0, 1)]
    for d in (0, 1):
        far[d].wait_recv()
        far[2 + d].wait_recv()
        for h in (0, 1):
            joined = OO[1 + d, :, half[h]] + OA[d, :, half[h]].astype(F32)
            if h == d:
                joined = joined + OH[d].astype(F32)
            OC[d, :, half[h]] = joined.astype(BF16)
        near.append(o_send(6 + d, OC.at[d], OR.at[2 + d], 2 - 4 * d))
    total = OO[0]
    for n in range(4):
        near[n].wait_recv()
        total = total + OR[n].astype(F32)
    out[...] = total
    for cp in started:
        cp.wait_send()


def body(orbitals, targets, coulomb):
    any_, dma = pl.BlockSpec(memory_space=pl.ANY), pltpu.SemaphoreType.DMA
    return pl.pallas_call(
        kernel,
        out_shape=jax.ShapeDtypeStruct((16, NB), F32),
        in_specs=[any_] * 3,
        out_specs=pl.BlockSpec(memory_space=pltpu.VMEM),
        scratch_shapes=[
            pltpu.VMEM((16, 8 * KS), BF16),
            pltpu.VMEM((8, 4, 2, 16, KS), BF16),
            pltpu.VMEM((8, 4, 2, 16, KS), BF16),
            pltpu.VMEM((8, 4, 2, 16, NB), BF16),
            pltpu.VMEM((8, 4, 16, 1024), BF16),
            pltpu.VMEM((8, 4, 16, 1024), BF16),
            pltpu.VMEM((8, 4, 16, 1024), F32),
            pltpu.VMEM((2, 8, 16, 1024), BF16),
            pltpu.VMEM((2, 8, 16, 1024), BF16),
            pltpu.VMEM((2, 8, 16, 1024), BF16),
            pltpu.VMEM((2, 8, 16, 1024), BF16),
            pltpu.VMEM((512, 256), F32),
            pltpu.VMEM((4, 2, 8, 16, 128), BF16),
            pltpu.VMEM((4, 2, 8, 16, 128), BF16),
            pltpu.VMEM((8, 16, 1024), BF16),
            pltpu.VMEM((8, 16, NB), BF16),
            pltpu.VMEM((2, 16, NB), BF16),
            pltpu.VMEM((2, 16, NB // 2), BF16),
            pltpu.VMEM((2, 16, NB), BF16),
            pltpu.VMEM((4, 16, NB), BF16),
            pltpu.VMEM((3, 16, NB), F32),
            dma((9,)),
            dma((7,)), dma((7,)),
            dma((64,)), dma((64,)),
            dma((16,)), dma((16,)),
            dma((3,)), dma((3,)),
            dma((5,)), dma((5,)),
            dma((20,)), dma((20,)),
            dma((8,)), dma((8,)),
        ],
        compiler_params=pltpu.CompilerParams(
            collective_id=0, has_side_effects=True, vmem_limit_bytes=60 * 1024 * 1024
        ),
        cost_estimate=pl.CostEstimate(flops=2_500_000_000, bytes_accessed=4_000_000, transcendentals=0),
    )(orbitals, targets, coulomb)


def solution(mesh):
    in_specs = (P(("row", "col"), None), P(("row", "col"), None), P("row", "col"))
    return jax.shard_map(
        body, mesh=mesh, in_specs=in_specs, out_specs=P(("row", "col"), None), check_vma=False
    )
```

```python
import functools

import jax
import jax.numpy as jnp
from jax import lax
from jax.experimental import pallas as pl
from jax.experimental.pallas import tpu as pltpu
from jax.sharding import PartitionSpec as P

MESH = pl.DeviceIdType.MESH
F32 = jnp.float32
BF16 = jnp.bfloat16
KS = 1024
NB = 1024

SLOT = {4: 0, 0: 1, 1: 2, -1: 3, 2: 4, -2: 5, 3: 6, -3: 7, -4: 0}
OFFSET = (4, 0, 1, -1, 2, -2, 3, -3)
RECTS = ((1, 6, 1, 6), (6, 8, 1, 8), (1, 6, 6, 8), (0, 1, 1, 8), (0, 8, 0, 1))
HALVES = (
    ((slice(1, 4), slice(128, 768)), (slice(4, 6), slice(128, 768))),
    ((slice(6, 7), slice(128, 1024)), (slice(7, 8), slice(128, 1024))),
    ((slice(1, 6), slice(768, 896)), (slice(1, 6), slice(896, 1024))),
)
DX = (0, 1, 3, 2)


def kernel(
    orb, tgt, cou, out,
    W, A, B, T, SB, RB, OWN, XS, XR, YS, YR, VF, VB, VR, S, OB, OA, OH, OC, OR, OO,
    loc, a_s, a_r, g_s, g_r, t_s, t_r, v_s, v_r, d_s, d_r, x_s, x_r, o_s, o_r,
):
    row, col = lax.axis_index("row"), lax.axis_index("col")
    x, yh, c = lax.div(row, 4), lax.rem(lax.div(row, 2), 2), lax.rem(row, 2)
    yl, z = lax.div(col, 8), lax.rem(col, 8)
    y = yh * 4 + yl
    sib = 1 - c

    def dev(x_, y_, z_, c_):
        return ((x_ * 2 + lax.div(y_, 4)) * 2 + c_, lax.rem(y_, 4) * 8 + z_)

    def at(dx=0, dy=0, dz=0, dc=0):
        return dev(
            lax.rem(x + dx + 4, 4), lax.rem(y + dy + 8, 8), lax.rem(z + dz + 8, 8), sib if dc else c
        )

    def yl_peer(d):
        return (row, lax.rem(yl + d, 4) * 8 + z)

    started = []
    tr = {}

    def remote(src, dst, ss, rs, to):
        return pltpu.make_async_remote_copy(
            src_ref=src, dst_ref=dst, send_sem=ss, recv_sem=rs, device_id=to, device_id_type=MESH
        )

    def go(cp):
        cp.start()
        started.append(cp)
        return cp

    def own_slice(ref, g):
        return ref.at[:, pl.ds(pl.multiple_of(g * KS, KS), KS)]

    w_in = pltpu.make_async_copy(orb, W, loc.at[8])
    w_in.start()
    v_in = pltpu.make_async_copy(cou, VF, loc.at[0])
    v_in.start()
    t_in = pltpu.make_async_copy(tgt, T.at[1, x, c], loc.at[1])
    t_in.start()
    a_in = pltpu.make_async_copy(own_slice(orb, x * 2 + c), A.at[1, x, c], loc.at[2])
    a_in.start()

    barrier = pltpu.get_barrier_semaphore()
    partners = [at(dx=dx, dc=dc) for dx in range(4) for dc in range(2) if dx or dc]
    partners += [at(dy=d) for d in (1, -1, 2, -2)] + [at(dz=d) for d in (1, -1, 2, -2)] + [yl_peer(d) for d in (1, 2, 3)]
    for p in partners:
        pl.semaphore_signal(barrier, inc=1, device_id=p, device_id_type=MESH)
    pl.semaphore_wait(barrier, len(partners))

    def t_send(n, d, src, dst, cols, far):
        cp = remote(
            T.at[SLOT[src], x, c, :, cols], T.at[SLOT[dst], x, c, :, cols], t_s.at[n], t_r.at[n],
            at(dy=far * (1 - 2 * d)),
        )
        tr[n] = go(cp)

    whole, half = slice(0, NB), (slice(0, NB // 2), slice(NB // 2, NB))

    def t_start():
        for d in (0, 1):
            sg = 2 * d - 1
            t_send(d, d, 0, 2 * sg, whole, 2)
            t_send(2 + d, d, 0, sg, whole, 1)

    def t_on():
        for d in (0, 1):
            sg = 2 * d - 1
            tr[d].wait_recv()
            t_send(4 + d, d, 2 * sg, 3 * sg, whole, 1)
            t_send(6 + d, d, 2 * sg, 4 * sg, half[d], 2)

    swaps = {}
    w_in.wait()
    t_in.wait()
    for i, dx in enumerate(DX):
        for dc in (1, 0):
            if dx or dc:
                n = dx * 2 + dc - 1
                xp = lax.rem(x + dx, 4)
                cp_ = sib if dc else c
                swaps[dx, dc] = go(
                    remote(own_slice(W, xp * 2 + cp_), A.at[1, x, c], a_s.at[n], a_r.at[n], at(dx=dx, dc=dc))
                )

    t_start()

    chunk = [lax.rem(x - dx + 4, 4) for dx in DX]

    def ring(kind, d, s, i):
        sg = -1 if d == 0 else 1
        buf = B if kind else A
        src = A if s == 1 else buf
        n = ((kind * 2 + d) * 4 + s - 1) * 4 + i
        to = at(dy=-sg) if kind else at(dz=-sg)
        return remote(
            src.at[SLOT[sg * (s - 1)], chunk[i]], buf.at[SLOT[sg * s], chunk[i]], g_s.at[n], g_r.at[n], to
        )

    rg = {}

    def forward(s, i, kinds=(0, 1)):
        for kind in kinds:
            for d in (0, 1):
                if s > 1:
                    rg[kind, d, s - 1, i].wait_recv()
                if s < 4 or (d == 0) == (i < 2):
                    rg[kind, d, s, i] = go(ring(kind, d, s, i))

    b_own = []
    for i, dx in enumerate(DX):
        if dx == 0:
            a_in.wait()
            swaps[0, 1].wait_recv()
        else:
            swaps[dx, 0].wait_recv()
            swaps[dx, 1].wait_recv()
        forward(1, i)
        cp = pltpu.make_async_copy(A.at[1, chunk[i]], B.at[1, chunk[i]], loc.at[3 + i])
        cp.start()
        b_own.append(cp)
    t_on()

    v_in.wait()
    dst = lax.broadcasted_iota(jnp.int32, (256, 256), 1)
    src = lax.broadcasted_iota(jnp.int32, (256, 256), 0)
    want = ((dst & 127) >> 5) * 64 + (dst >> 7) * 32 + (dst & 31)
    perm = jnp.where(src == want, 1.0, 0.0).astype(BF16)
    for q in range(4):
        moved = jnp.dot(VF[q * 128:(q + 1) * 128, :].astype(BF16), perm, preferred_element_type=F32).astype(BF16)
        VB[q, 0] = moved[:, :128].reshape(8, 16, 128)
        VB[q, 1] = moved[:, 128:].reshape(8, 16, 128)
    v_own = pltpu.make_async_copy(VB.at[yl], VR.at[yl], loc.at[7])
    v_own.start()

    dd, xx = {}, {}

    def compute(n):
        r0, r1, c0, c1 = RECTS[n]
        rows = (r1 - r0) * 64
        left = jnp.concatenate(
            [A[r0:r1, :, sib].reshape(rows, KS), A[r0:r1, :, c].reshape(rows, KS)], axis=0
        )
        q = c0
        while q < c1:
            w = min(2 - (q & 1), c1 - q)
            right = B[q:q + w].reshape(w * 128, KS)
            tile = lax.dot_general(left, right, (((1,), (1,)), ((), ())), preferred_element_type=F32)
            tile = tile.reshape(2, r1 - r0, 4, 16, w * 128)
            cols = slice(q * 128, (q + w) * 128)
            SB[r0:r1, :, :, cols] = tile[0].astype(BF16)
            OWN[r0:r1, :, :, cols] = tile[1]
            q += w
        where = (slice(r0, r1), slice(None), slice(None), slice(c0 * 128, c1 * 128))
        dd[n] = go(remote(SB.at[where], RB.at[where], d_s.at[n], d_r.at[n], at(dc=1)))

    xm, xp1, xf = lax.rem(x + 3, 4), lax.rem(x + 1, 4), lax.rem(x + 2, 4)

    def x_send(n, k, src, dst, d, rows, cols):
        where = (d, rows, slice(None), cols)
        xx[n, k, d] = go(
            remote(src.at[where], dst.at[where], x_s.at[n * 4 + k * 2 + d], x_r.at[n * 4 + k * 2 + d], at(dx=1 - 2 * d))
        )

    def spread(n):
        dd[n].wait_recv()
        for d in (0, 1):
            rows, cols = HALVES[n][d]
            for r in range(rows.start, rows.stop):
                XS[d, r, :, cols] = (OWN[r, xf, :, cols] + RB[r, xf, :, cols].astype(F32)).astype(BF16)
            x_send(n, 0, XS, XR, d, rows, cols)

    def combine(n):
        r0, r1, c0, c1 = RECTS[n]
        for d in (0, 1):
            xx[n, 0, d].wait_recv()
            to = xm if d else xp1
            for h in (0, 1):
                rows, cols = HALVES[n][h]
                for r in range(rows.start, rows.stop):
                    part = OWN[r, to, :, cols] + RB[r, to, :, cols].astype(F32)
                    if h == d:
                        part = part + XR[d, r, :, cols].astype(F32)
                    YS[d, r, :, cols] = part.astype(BF16)
            x_send(n, 1, YS, YR, d, slice(r0, r1), slice(c0 * 128, c1 * 128))

    def direct(n):
        r0, r1, c0, c1 = RECTS[n]
        rows, cols = slice(r0, r1), slice(c0 * 128, c1 * 128)
        dd[n].wait_recv()
        for k, buf, land, to, dx in ((2, XS, XR, xf, 2), (0, YS, YR, xp1, 1), (1, YS, YR, xm, -1)):
            j = k % 2
            for r in range(r0, r1):
                buf[j, r, :, cols] = (OWN[r, to, :, cols] + RB[r, to, :, cols].astype(F32)).astype(BF16)
            where = (j, rows, slice(None), cols)
            m = n * 4 + k
            xx[n, 1, k] = go(remote(buf.at[where], land.at[where], x_s.at[m], x_r.at[m], at(dx=dx)))

    def finish(n):
        r0, r1, c0, c1 = RECTS[n]
        for d in (0, 1, 2):
            if (n, 1, d) in xx:
                xx[n, 1, d].wait_recv()
        for q in range(c0, c1):
            yq = lax.rem(y + OFFSET[q] + 8, 8)
            cols = slice(q * 128, (q + 1) * 128)
            for r in range(r0, r1):
                zr = lax.rem(z + OFFSET[r] + 8, 8)
                pairs = OWN[r, x, :, cols] + RB[r, x, :, cols].astype(F32)
                for d in (0, 1):
                    pairs = pairs + YR[d, r, :, cols].astype(F32)
                if n > 2:
                    pairs = pairs + XR[0, r, :, cols].astype(F32)
                v = VR[lax.rem(yq, 4), lax.div(yq, 4), zr].astype(F32)
                S[r, :, cols] = (pairs * v).astype(BF16)

    tx, td = {}, {}

    def t_sib(k, xv):
        td[k] = go(remote(T.at[:, xv, c], T.at[:, xv, c], t_s.at[12 + k], t_r.at[12 + k], at(dc=1)))

    def t_first():
        for n in range(2, 8):
            tr[n].wait_recv()
        tx[0] = go(remote(T.at[:, x, c], T.at[:, x, c], t_s.at[8], t_r.at[8], at(dx=1)))
        tx[1] = go(remote(T.at[:, x, c], T.at[:, x, c], t_s.at[9], t_r.at[9], at(dx=-1)))
        t_sib(0, x)

    def t_second():
        tx[0].wait_recv()
        tx[2] = go(remote(T.at[0:4, xm, c], T.at[0:4, xm, c], t_s.at[10], t_r.at[10], at(dx=1)))
        tx[1].wait_recv()
        tx[3] = go(remote(T.at[4:8, xp1, c], T.at[4:8, xp1, c], t_s.at[11], t_r.at[11], at(dx=-1)))
        t_sib(1, xm)
        t_sib(2, xp1)

    def t_third():
        tx[2].wait_recv()
        tx[3].wait_recv()
        t_sib(3, xf)

    for i in range(4):
        forward(2, i)
    t_first()
    for i in range(4):
        forward(3, i)
    for cp in b_own:
        cp.wait()
    compute(0)
    for i in range(4):
        forward(4, i)
        if i == 0:
            spread(0)
            t_second()
    compute(1)
    compute(2)
    combine(0)
    spread(1)
    spread(2)
    for i in range(4):
        rg[0, i // 2, 4, i].wait_recv()
    compute(3)
    for i in range(4):
        rg[1, i // 2, 4, i].wait_recv()
    v_out = []
    for d in (1, 2, 3):
        v_out.append(
            go(remote(VB.at[lax.rem(yl + d, 4)], VR.at[yl], v_s.at[d - 1], v_r.at[d - 1], yl_peer(d)))
        )
    compute(4)
    direct(3)
    direct(4)
    combine(1)
    combine(2)
    t_third()
    v_own.wait()
    for cp in v_out:
        cp.wait_recv()
    for n in range(5):
        finish(n)
    for k in range(4):
        td[k].wait_recv()

    left = S[...].reshape(128, 1024)
    for q in range(4):
        cols = slice(q * 256, (q + 1) * 256)
        part = jnp.dot(left, T[:, :, :, :, cols].reshape(1024, 256), preferred_element_type=F32)
        part = part.reshape(8, 16, 256)
        for k in range(3):
            OO[k, :, cols] = part[SLOT[(0, 2, -2)[k]]]
        OB[:, :, cols] = part.astype(BF16)

    def o_send(n, src, dst, dz):
        return go(remote(src, dst, o_s.at[n], o_r.at[n], at(dz=dz)))

    far = [o_send(d, OB.at[0, :, half[d]], OH.at[d], 2 - 4 * d) for d in (0, 1)]
    far += [o_send(2 + d, OB.at[SLOT[3 - 6 * d]], OA.at[d], 1 - 2 * d) for d in (0, 1)]
    near = [o_send(4 + d, OB.at[SLOT[1 - 2 * d]], OR.at[d], 1 - 2 * d) for d in (0, 1)]
    for d in (0, 1):
        far[d].wait_recv()
        far[2 + d].wait_recv()
        for h in (0, 1):
            joined = OO[1 + d, :, half[h]] + OA[d, :, half[h]].astype(F32)
            if h == d:
                joined = joined + OH[d].astype(F32)
            OC[d, :, half[h]] = joined.astype(BF16)
        near.append(o_send(6 + d, OC.at[d], OR.at[2 + d], 2 - 4 * d))
    total = OO[0]
    for n in range(4):
        near[n].wait_recv()
        total = total + OR[n].astype(F32)
    out[...] = total
    for cp in started:
        cp.wait_send()


def body(orbitals, targets, coulomb):
    any_, dma = pl.BlockSpec(memory_space=pl.ANY), pltpu.SemaphoreType.DMA
    return pl.pallas_call(
        kernel,
        out_shape=jax.ShapeDtypeStruct((16, NB), F32),
        in_specs=[any_] * 3,
        out_specs=pl.BlockSpec(memory_space=pltpu.VMEM),
        scratch_shapes=[
            pltpu.VMEM((16, 8 * KS), BF16),
            pltpu.VMEM((8, 4, 2, 16, KS), BF16),
            pltpu.VMEM((8, 4, 2, 16, KS), BF16),
            pltpu.VMEM((8, 4, 2, 16, NB), BF16),
            pltpu.VMEM((8, 4, 16, 1024), BF16),
            pltpu.VMEM((8, 4, 16, 1024), BF16),
            pltpu.VMEM((8, 4, 16, 1024), F32),
            pltpu.VMEM((2, 8, 16, 1024), BF16),
            pltpu.VMEM((2, 8, 16, 1024), BF16),
            pltpu.VMEM((2, 8, 16, 1024), BF16),
            pltpu.VMEM((2, 8, 16, 1024), BF16),
            pltpu.VMEM((512, 256), F32),
            pltpu.VMEM((4, 2, 8, 16, 128), BF16),
            pltpu.VMEM((4, 2, 8, 16, 128), BF16),
            pltpu.VMEM((8, 16, 1024), BF16),
            pltpu.VMEM((8, 16, NB), BF16),
            pltpu.VMEM((2, 16, NB), BF16),
            pltpu.VMEM((2, 16, NB // 2), BF16),
            pltpu.VMEM((2, 16, NB), BF16),
            pltpu.VMEM((4, 16, NB), BF16),
            pltpu.VMEM((3, 16, NB), F32),
            dma((9,)),
            dma((7,)), dma((7,)),
            dma((64,)), dma((64,)),
            dma((16,)), dma((16,)),
            dma((3,)), dma((3,)),
            dma((5,)), dma((5,)),
            dma((20,)), dma((20,)),
            dma((8,)), dma((8,)),
        ],
        compiler_params=pltpu.CompilerParams(
            collective_id=0, has_side_effects=True, vmem_limit_bytes=55040 * 1024
        ),
        cost_estimate=pl.CostEstimate(flops=2_500_000_000, bytes_accessed=4_000_000, transcendentals=0),
    )(orbitals, targets, coulomb)


def solution(mesh):
    in_specs = (P(("row", "col"), None), P(("row", "col"), None), P("row", "col"))
    return jax.shard_map(
        body, mesh=mesh, in_specs=in_specs, out_specs=P(("row", "col"), None), check_vma=False
    )
```

```python
import functools

import jax
import jax.numpy as jnp
from jax import lax
from jax.experimental import pallas as pl
from jax.experimental.pallas import tpu as pltpu
from jax.sharding import PartitionSpec as P

MESH = pl.DeviceIdType.MESH
F32 = jnp.float32
BF16 = jnp.bfloat16
KS = 1024
NB = 1024

SLOT = {4: 0, 0: 1, 1: 2, -1: 3, 2: 4, -2: 5, 3: 6, -3: 7, -4: 0}
OFFSET = (4, 0, 1, -1, 2, -2, 3, -3)
RECTS = ((1, 6, 1, 6), (6, 8, 1, 8), (1, 6, 6, 8), (0, 1, 1, 8), (0, 8, 0, 1))
HALVES = (
    ((slice(1, 4), slice(128, 768)), (slice(4, 6), slice(128, 768))),
    ((slice(6, 7), slice(128, 1024)), (slice(7, 8), slice(128, 1024))),
    ((slice(1, 6), slice(768, 896)), (slice(1, 6), slice(896, 1024))),
)
DX = (0, 1, 3, 2)
ORDER = ((0, 1, 2, 3), (0, 2, 3, 1))


def kernel(
    orb, tgt, cou, out,
    W, A, B, T, SB, RB, OWN, XS, XR, YS, YR, VF, VB, VR, S, OB, OA, OH, OC, OR, OO,
    loc, a_s, a_r, g_s, g_r, t_s, t_r, v_s, v_r, d_s, d_r, x_s, x_r, o_s, o_r,
):
    row, col = lax.axis_index("row"), lax.axis_index("col")
    x, yh, c = lax.div(row, 4), lax.rem(lax.div(row, 2), 2), lax.rem(row, 2)
    yl, z = lax.div(col, 8), lax.rem(col, 8)
    y = yh * 4 + yl
    sib = 1 - c

    def dev(x_, y_, z_, c_):
        return ((x_ * 2 + lax.div(y_, 4)) * 2 + c_, lax.rem(y_, 4) * 8 + z_)

    def at(dx=0, dy=0, dz=0, dc=0):
        return dev(
            lax.rem(x + dx + 4, 4), lax.rem(y + dy + 8, 8), lax.rem(z + dz + 8, 8), sib if dc else c
        )

    def yl_peer(d):
        return (row, lax.rem(yl + d, 4) * 8 + z)

    started = []
    tr = {}

    def remote(src, dst, ss, rs, to):
        return pltpu.make_async_remote_copy(
            src_ref=src, dst_ref=dst, send_sem=ss, recv_sem=rs, device_id=to, device_id_type=MESH
        )

    def go(cp):
        cp.start()
        started.append(cp)
        return cp

    def own_slice(ref, g):
        return ref.at[:, pl.ds(pl.multiple_of(g * KS, KS), KS)]

    w_in = pltpu.make_async_copy(orb, W, loc.at[8])
    w_in.start()
    v_in = pltpu.make_async_copy(cou, VF, loc.at[0])
    v_in.start()
    t_in = pltpu.make_async_copy(tgt, T.at[1, x, c], loc.at[1])
    t_in.start()
    a_in = pltpu.make_async_copy(own_slice(orb, x * 2 + c), A.at[1, x, c], loc.at[2])
    a_in.start()

    barrier = pltpu.get_barrier_semaphore()
    partners = [at(dx=dx, dc=dc) for dx in range(4) for dc in range(2) if dx or dc]
    partners += [at(dy=d) for d in (1, -1, 2, -2)] + [at(dz=d) for d in (1, -1, 2, -2)] + [yl_peer(d) for d in (1, 2, 3)]
    for p in partners:
        pl.semaphore_signal(barrier, inc=1, device_id=p, device_id_type=MESH)
    pl.semaphore_wait(barrier, len(partners))

    def t_send(n, d, src, dst, cols, far):
        cp = remote(
            T.at[SLOT[src], x, c, :, cols], T.at[SLOT[dst], x, c, :, cols], t_s.at[n], t_r.at[n],
            at(dy=far * (1 - 2 * d)),
        )
        tr[n] = go(cp)

    whole, half = slice(0, NB), (slice(0, NB // 2), slice(NB // 2, NB))

    def t_start():
        for d in (0, 1):
            sg = 2 * d - 1
            t_send(d, d, 0, 2 * sg, whole, 2)
            t_send(2 + d, d, 0, sg, whole, 1)

    def t_on():
        for d in (0, 1):
            sg = 2 * d - 1
            tr[d].wait_recv()
            t_send(4 + d, d, 2 * sg, 3 * sg, whole, 1)
            t_send(6 + d, d, 2 * sg, 4 * sg, half[d], 2)

    swaps = {}
    w_in.wait()
    t_in.wait()
    for i, dx in enumerate(DX):
        for dc in (1, 0):
            if dx or dc:
                n = dx * 2 + dc - 1
                xp = lax.rem(x + dx, 4)
                cp_ = sib if dc else c
                swaps[dx, dc] = go(
                    remote(own_slice(W, xp * 2 + cp_), A.at[1, x, c], a_s.at[n], a_r.at[n], at(dx=dx, dc=dc))
                )

    t_start()

    chunk = [lax.rem(x - dx + 4, 4) for dx in DX]

    def ring(kind, d, s, i):
        sg = -1 if d == 0 else 1
        buf = B if kind else A
        src = A if s == 1 else buf
        n = ((kind * 2 + d) * 4 + s - 1) * 4 + i
        to = at(dy=-sg) if kind else at(dz=-sg)
        return remote(
            src.at[SLOT[sg * (s - 1)], chunk[i]], buf.at[SLOT[sg * s], chunk[i]], g_s.at[n], g_r.at[n], to
        )

    rg = {}

    def forward(s, i, kinds=(0, 1)):
        for kind in kinds:
            for d in (0, 1):
                j = ORDER[d][i]
                if s > 1:
                    rg[kind, d, s - 1, j].wait_recv()
                if s < 4 or (d == 0) == (j < 2):
                    rg[kind, d, s, j] = go(ring(kind, d, s, j))

    b_own = []
    for i, dx in enumerate(DX):
        if dx == 0:
            a_in.wait()
            swaps[0, 1].wait_recv()
        for near in ((), (1, 3), (2,), ())[i]:
            swaps[near, 0].wait_recv()
            swaps[near, 1].wait_recv()
        forward(1, i)
        cp = pltpu.make_async_copy(A.at[1, chunk[i]], B.at[1, chunk[i]], loc.at[3 + i])
        cp.start()
        b_own.append(cp)
    t_on()

    v_in.wait()
    dst = lax.broadcasted_iota(jnp.int32, (256, 256), 1)
    src = lax.broadcasted_iota(jnp.int32, (256, 256), 0)
    want = ((dst & 127) >> 5) * 64 + (dst >> 7) * 32 + (dst & 31)
    perm = jnp.where(src == want, 1.0, 0.0).astype(BF16)
    for q in range(4):
        moved = jnp.dot(VF[q * 128:(q + 1) * 128, :].astype(BF16), perm, preferred_element_type=F32).astype(BF16)
        VB[q, 0] = moved[:, :128].reshape(8, 16, 128)
        VB[q, 1] = moved[:, 128:].reshape(8, 16, 128)
    v_own = pltpu.make_async_copy(VB.at[yl], VR.at[yl], loc.at[7])
    v_own.start()

    dd, xx = {}, {}

    def compute(n):
        r0, r1, c0, c1 = RECTS[n]
        rows = (r1 - r0) * 64
        left = jnp.concatenate(
            [A[r0:r1, :, sib].reshape(rows, KS), A[r0:r1, :, c].reshape(rows, KS)], axis=0
        )
        q = c0
        while q < c1:
            w = min(2 - (q & 1), c1 - q)
            right = B[q:q + w].reshape(w * 128, KS)
            tile = lax.dot_general(left, right, (((1,), (1,)), ((), ())), preferred_element_type=F32)
            tile = tile.reshape(2, r1 - r0, 4, 16, w * 128)
            cols = slice(q * 128, (q + w) * 128)
            SB[r0:r1, :, :, cols] = tile[0].astype(BF16)
            OWN[r0:r1, :, :, cols] = tile[1]
            q += w
        where = (slice(r0, r1), slice(None), slice(None), slice(c0 * 128, c1 * 128))
        dd[n] = go(remote(SB.at[where], RB.at[where], d_s.at[n], d_r.at[n], at(dc=1)))

    xm, xp1, xf = lax.rem(x + 3, 4), lax.rem(x + 1, 4), lax.rem(x + 2, 4)

    def x_send(n, k, src, dst, d, rows, cols):
        where = (d, rows, slice(None), cols)
        xx[n, k, d] = go(
            remote(src.at[where], dst.at[where], x_s.at[n * 4 + k * 2 + d], x_r.at[n * 4 + k * 2 + d], at(dx=1 - 2 * d))
        )

    def spread(n):
        dd[n].wait_recv()
        for d in (0, 1):
            rows, cols = HALVES[n][d]
            for r in range(rows.start, rows.stop):
                XS[d, r, :, cols] = (OWN[r, xf, :, cols] + RB[r, xf, :, cols].astype(F32)).astype(BF16)
            x_send(n, 0, XS, XR, d, rows, cols)

    def combine(n):
        r0, r1, c0, c1 = RECTS[n]
        for d in (0, 1):
            xx[n, 0, d].wait_recv()
            to = xm if d else xp1
            for h in (0, 1):
                rows, cols = HALVES[n][h]
                for r in range(rows.start, rows.stop):
                    part = OWN[r, to, :, cols] + RB[r, to, :, cols].astype(F32)
                    if h == d:
                        part = part + XR[d, r, :, cols].astype(F32)
                    YS[d, r, :, cols] = part.astype(BF16)
            x_send(n, 1, YS, YR, d, slice(r0, r1), slice(c0 * 128, c1 * 128))

    def direct(n):
        r0, r1, c0, c1 = RECTS[n]
        rows, cols = slice(r0, r1), slice(c0 * 128, c1 * 128)
        dd[n].wait_recv()
        for k, buf, land, to, dx in ((2, XS, XR, xf, 2), (0, YS, YR, xp1, 1), (1, YS, YR, xm, -1)):
            j = k % 2
            for r in range(r0, r1):
                buf[j, r, :, cols] = (OWN[r, to, :, cols] + RB[r, to, :, cols].astype(F32)).astype(BF16)
            where = (j, rows, slice(None), cols)
            m = n * 4 + k
            xx[n, 1, k] = go(remote(buf.at[where], land.at[where], x_s.at[m], x_r.at[m], at(dx=dx)))

    def finish(n):
        r0, r1, c0, c1 = RECTS[n]
        for d in (0, 1, 2):
            if (n, 1, d) in xx:
                xx[n, 1, d].wait_recv()
        for q in range(c0, c1):
            yq = lax.rem(y + OFFSET[q] + 8, 8)
            cols = slice(q * 128, (q + 1) * 128)
            for r in range(r0, r1):
                zr = lax.rem(z + OFFSET[r] + 8, 8)
                pairs = OWN[r, x, :, cols] + RB[r, x, :, cols].astype(F32)
                for d in (0, 1):
                    pairs = pairs + YR[d, r, :, cols].astype(F32)
                if n > 2:
                    pairs = pairs + XR[0, r, :, cols].astype(F32)
                v = VR[lax.rem(yq, 4), lax.div(yq, 4), zr].astype(F32)
                S[r, :, cols] = (pairs * v).astype(BF16)

    tx, td = {}, {}

    def t_sib(k, xv):
        td[k] = go(remote(T.at[:, xv, c], T.at[:, xv, c], t_s.at[12 + k], t_r.at[12 + k], at(dc=1)))

    def t_first():
        for n in range(2, 8):
            tr[n].wait_recv()
        tx[0] = go(remote(T.at[:, x, c], T.at[:, x, c], t_s.at[8], t_r.at[8], at(dx=1)))
        tx[1] = go(remote(T.at[:, x, c], T.at[:, x, c], t_s.at[9], t_r.at[9], at(dx=-1)))
        t_sib(0, x)

    def t_second():
        tx[0].wait_recv()
        tx[2] = go(remote(T.at[0:4, xm, c], T.at[0:4, xm, c], t_s.at[10], t_r.at[10], at(dx=1)))
        tx[1].wait_recv()
        tx[3] = go(remote(T.at[4:8, xp1, c], T.at[4:8, xp1, c], t_s.at[11], t_r.at[11], at(dx=-1)))
        t_sib(1, xm)
        t_sib(2, xp1)

    def t_third():
        tx[2].wait_recv()
        tx[3].wait_recv()
        t_sib(3, xf)

    for i in range(4):
        forward(2, i)
    t_first()
    for i in range(4):
        forward(3, i)
    for cp in b_own:
        cp.wait()
    compute(0)
    for i in range(4):
        forward(4, i)
        if i == 0:
            spread(0)
            t_second()
    compute(1)
    compute(2)
    combine(0)
    spread(1)
    spread(2)
    for i in range(4):
        rg[0, i // 2, 4, i].wait_recv()
    compute(3)
    for i in range(4):
        rg[1, i // 2, 4, i].wait_recv()
    v_out = []
    for d in (1, 2, 3):
        v_out.append(
            go(remote(VB.at[lax.rem(yl + d, 4)], VR.at[yl], v_s.at[d - 1], v_r.at[d - 1], yl_peer(d)))
        )
    compute(4)
    direct(3)
    direct(4)
    combine(1)
    combine(2)
    t_third()
    v_own.wait()
    for cp in v_out:
        cp.wait_recv()
    for n in range(5):
        finish(n)
    for k in range(4):
        td[k].wait_recv()

    left = S[...].reshape(128, 1024)
    for q in range(4):
        cols = slice(q * 256, (q + 1) * 256)
        part = jnp.dot(left, T[:, :, :, :, cols].reshape(1024, 256), preferred_element_type=F32)
        part = part.reshape(8, 16, 256)
        for k in range(3):
            OO[k, :, cols] = part[SLOT[(0, 2, -2)[k]]]
        OB[:, :, cols] = part.astype(BF16)

    def o_send(n, src, dst, dz):
        return go(remote(src, dst, o_s.at[n], o_r.at[n], at(dz=dz)))

    far = [o_send(d, OB.at[0, :, half[d]], OH.at[d], 2 - 4 * d) for d in (0, 1)]
    far += [o_send(2 + d, OB.at[SLOT[3 - 6 * d]], OA.at[d], 1 - 2 * d) for d in (0, 1)]
    near = [o_send(4 + d, OB.at[SLOT[1 - 2 * d]], OR.at[d], 1 - 2 * d) for d in (0, 1)]
    for d in (0, 1):
        far[d].wait_recv()
        far[2 + d].wait_recv()
        for h in (0, 1):
            joined = OO[1 + d, :, half[h]] + OA[d, :, half[h]].astype(F32)
            if h == d:
                joined = joined + OH[d].astype(F32)
            OC[d, :, half[h]] = joined.astype(BF16)
        near.append(o_send(6 + d, OC.at[d], OR.at[2 + d], 2 - 4 * d))
    total = OO[0]
    for n in range(4):
        near[n].wait_recv()
        total = total + OR[n].astype(F32)
    out[...] = total
    for cp in started:
        cp.wait_send()


def body(orbitals, targets, coulomb):
    any_, dma = pl.BlockSpec(memory_space=pl.ANY), pltpu.SemaphoreType.DMA
    return pl.pallas_call(
        kernel,
        out_shape=jax.ShapeDtypeStruct((16, NB), F32),
        in_specs=[any_] * 3,
        out_specs=pl.BlockSpec(memory_space=pltpu.VMEM),
        scratch_shapes=[
            pltpu.VMEM((16, 8 * KS), BF16),
            pltpu.VMEM((8, 4, 2, 16, KS), BF16),
            pltpu.VMEM((8, 4, 2, 16, KS), BF16),
            pltpu.VMEM((8, 4, 2, 16, NB), BF16),
            pltpu.VMEM((8, 4, 16, 1024), BF16),
            pltpu.VMEM((8, 4, 16, 1024), BF16),
            pltpu.VMEM((8, 4, 16, 1024), F32),
            pltpu.VMEM((2, 8, 16, 1024), BF16),
            pltpu.VMEM((2, 8, 16, 1024), BF16),
            pltpu.VMEM((2, 8, 16, 1024), BF16),
            pltpu.VMEM((2, 8, 16, 1024), BF16),
            pltpu.VMEM((512, 256), F32),
            pltpu.VMEM((4, 2, 8, 16, 128), BF16),
            pltpu.VMEM((4, 2, 8, 16, 128), BF16),
            pltpu.VMEM((8, 16, 1024), BF16),
            pltpu.VMEM((8, 16, NB), BF16),
            pltpu.VMEM((2, 16, NB), BF16),
            pltpu.VMEM((2, 16, NB // 2), BF16),
            pltpu.VMEM((2, 16, NB), BF16),
            pltpu.VMEM((4, 16, NB), BF16),
            pltpu.VMEM((3, 16, NB), F32),
            dma((9,)),
            dma((7,)), dma((7,)),
            dma((64,)), dma((64,)),
            dma((16,)), dma((16,)),
            dma((3,)), dma((3,)),
            dma((5,)), dma((5,)),
            dma((20,)), dma((20,)),
            dma((8,)), dma((8,)),
        ],
        compiler_params=pltpu.CompilerParams(
            collective_id=0, has_side_effects=True, vmem_limit_bytes=55040 * 1024
        ),
        cost_estimate=pl.CostEstimate(flops=2_500_000_000, bytes_accessed=4_000_000, transcendentals=0),
    )(orbitals, targets, coulomb)


def solution(mesh):
    in_specs = (P(("row", "col"), None), P(("row", "col"), None), P("row", "col"))
    return jax.shard_map(
        body, mesh=mesh, in_specs=in_specs, out_specs=P(("row", "col"), None), check_vma=False
    )
```

```python
import functools

import jax
import jax.numpy as jnp
from jax import lax
from jax.experimental import pallas as pl
from jax.experimental.pallas import tpu as pltpu
from jax.sharding import PartitionSpec as P

MESH = pl.DeviceIdType.MESH
F32 = jnp.float32
BF16 = jnp.bfloat16
KS = 1024
NB = 1024

SLOT = {4: 0, 0: 1, 1: 2, -1: 3, 2: 4, -2: 5, 3: 6, -3: 7, -4: 0}
OFFSET = (4, 0, 1, -1, 2, -2, 3, -3)
RECTS = ((1, 6, 1, 6), (6, 8, 1, 8), (1, 6, 6, 8), (0, 1, 1, 8), (0, 8, 0, 1))
HALVES = (
    ((slice(1, 4), slice(128, 768)), (slice(4, 6), slice(128, 768))),
    ((slice(6, 7), slice(128, 1024)), (slice(7, 8), slice(128, 1024))),
    ((slice(1, 6), slice(768, 896)), (slice(1, 6), slice(896, 1024))),
)
DX = (0, 1, 3, 2)
ORDER = ((0, 1, 2, 3), (0, 2, 3, 1))


def kernel(
    orb, tgt, cou, out,
    W, A, B, T, SB, RB, OWN, XS, XR, YS, YR, VF, VB, VR, S, OB, OA, OH, OC, OR, OO,
    loc, a_s, a_r, g_s, g_r, t_s, t_r, v_s, v_r, d_s, d_r, x_s, x_r, o_s, o_r,
):
    row, col = lax.axis_index("row"), lax.axis_index("col")
    x, yh, c = lax.div(row, 4), lax.rem(lax.div(row, 2), 2), lax.rem(row, 2)
    yl, z = lax.div(col, 8), lax.rem(col, 8)
    y = yh * 4 + yl
    sib = 1 - c

    def dev(x_, y_, z_, c_):
        return ((x_ * 2 + lax.div(y_, 4)) * 2 + c_, lax.rem(y_, 4) * 8 + z_)

    def at(dx=0, dy=0, dz=0, dc=0):
        return dev(
            lax.rem(x + dx + 4, 4), lax.rem(y + dy + 8, 8), lax.rem(z + dz + 8, 8), sib if dc else c
        )

    def yl_peer(d):
        return (row, lax.rem(yl + d, 4) * 8 + z)

    started = []
    tr = {}

    def remote(src, dst, ss, rs, to):
        return pltpu.make_async_remote_copy(
            src_ref=src, dst_ref=dst, send_sem=ss, recv_sem=rs, device_id=to, device_id_type=MESH
        )

    def go(cp):
        cp.start()
        started.append(cp)
        return cp

    def own_slice(ref, g):
        return ref.at[:, pl.ds(pl.multiple_of(g * KS, KS), KS)]

    w_in = pltpu.make_async_copy(orb, W, loc.at[8])
    w_in.start()
    v_in = pltpu.make_async_copy(cou, VF, loc.at[0])
    v_in.start()
    t_in = pltpu.make_async_copy(tgt, T.at[1, x, c], loc.at[1])
    t_in.start()
    a_in = pltpu.make_async_copy(own_slice(orb, x * 2 + c), A.at[1, x, c], loc.at[2])
    a_in.start()

    barrier = pltpu.get_barrier_semaphore()
    partners = [at(dx=dx, dc=dc) for dx in range(4) for dc in range(2) if dx or dc]
    partners += [at(dy=d) for d in (1, -1, 2, -2)] + [at(dz=d) for d in (1, -1, 2, -2)] + [yl_peer(d) for d in (1, 2, 3)]
    for p in partners:
        pl.semaphore_signal(barrier, inc=1, device_id=p, device_id_type=MESH)
    pl.semaphore_wait(barrier, len(partners))

    def t_send(n, d, src, dst, cols, far):
        cp = remote(
            T.at[SLOT[src], x, c, :, cols], T.at[SLOT[dst], x, c, :, cols], t_s.at[n], t_r.at[n],
            at(dy=far * (1 - 2 * d)),
        )
        tr[n] = go(cp)

    whole, half = slice(0, NB), (slice(0, NB // 2), slice(NB // 2, NB))

    def t_start():
        for d in (0, 1):
            sg = 2 * d - 1
            t_send(d, d, 0, 2 * sg, whole, 2)
            t_send(2 + d, d, 0, sg, whole, 1)

    def t_on():
        for d in (0, 1):
            sg = 2 * d - 1
            tr[d].wait_recv()
            t_send(4 + d, d, 2 * sg, 3 * sg, whole, 1)
            t_send(6 + d, d, 2 * sg, 4 * sg, half[d], 2)

    swaps = {}
    w_in.wait()
    t_in.wait()
    for i, dx in enumerate(DX):
        for dc in (1, 0):
            if dx or dc:
                n = dx * 2 + dc - 1
                xp = lax.rem(x + dx, 4)
                cp_ = sib if dc else c
                swaps[dx, dc] = go(
                    remote(own_slice(W, xp * 2 + cp_), A.at[1, x, c], a_s.at[n], a_r.at[n], at(dx=dx, dc=dc))
                )

    t_start()

    chunk = [lax.rem(x - dx + 4, 4) for dx in DX]

    def ring(kind, d, s, i):
        sg = -1 if d == 0 else 1
        buf = B if kind else A
        src = A if s == 1 else buf
        n = ((kind * 2 + d) * 4 + s - 1) * 4 + i
        to = at(dy=-sg) if kind else at(dz=-sg)
        return remote(
            src.at[SLOT[sg * (s - 1)], chunk[i]], buf.at[SLOT[sg * s], chunk[i]], g_s.at[n], g_r.at[n], to
        )

    rg = {}

    def forward(s, i, kinds=(0, 1)):
        for kind in kinds:
            for d in (0, 1):
                j = ORDER[d][i]
                if s > 1:
                    rg[kind, d, s - 1, j].wait_recv()
                if s < 4 or (d == 0) == (j < 2):
                    rg[kind, d, s, j] = go(ring(kind, d, s, j))

    b_own = []
    for i, dx in enumerate(DX):
        if dx == 0:
            a_in.wait()
            swaps[0, 1].wait_recv()
        for near in ((), (1, 3), (2,), ())[i]:
            swaps[near, 0].wait_recv()
            swaps[near, 1].wait_recv()
        forward(1, i)
        cp = pltpu.make_async_copy(A.at[1, chunk[i]], B.at[1, chunk[i]], loc.at[3 + i])
        cp.start()
        b_own.append(cp)
    t_on()

    v_in.wait()
    dst = lax.broadcasted_iota(jnp.int32, (256, 256), 1)
    src = lax.broadcasted_iota(jnp.int32, (256, 256), 0)
    want = ((dst & 127) >> 5) * 64 + (dst >> 7) * 32 + (dst & 31)
    perm = jnp.where(src == want, 1.0, 0.0).astype(BF16)
    for q in range(4):
        moved = jnp.dot(VF[q * 128:(q + 1) * 128, :].astype(BF16), perm, preferred_element_type=F32).astype(BF16)
        VB[q, 0] = moved[:, :128].reshape(8, 16, 128)
        VB[q, 1] = moved[:, 128:].reshape(8, 16, 128)
    v_own = pltpu.make_async_copy(VB.at[yl], VR.at[yl], loc.at[7])
    v_own.start()

    dd, xx = {}, {}

    def compute(n):
        r0, r1, c0, c1 = RECTS[n]
        rows = (r1 - r0) * 64
        left = jnp.concatenate(
            [A[r0:r1, :, sib].reshape(rows, KS), A[r0:r1, :, c].reshape(rows, KS)], axis=0
        )
        q = c0
        while q < c1:
            w = min(2 - (q & 1), c1 - q)
            right = B[q:q + w].reshape(w * 128, KS)
            tile = lax.dot_general(left, right, (((1,), (1,)), ((), ())), preferred_element_type=F32)
            tile = tile.reshape(2, r1 - r0, 4, 16, w * 128)
            cols = slice(q * 128, (q + w) * 128)
            SB[r0:r1, :, :, cols] = tile[0].astype(BF16)
            OWN[r0:r1, :, :, cols] = tile[1]
            q += w
        where = (slice(r0, r1), slice(None), slice(None), slice(c0 * 128, c1 * 128))
        dd[n] = go(remote(SB.at[where], RB.at[where], d_s.at[n], d_r.at[n], at(dc=1)))

    xm, xp1, xf = lax.rem(x + 3, 4), lax.rem(x + 1, 4), lax.rem(x + 2, 4)

    def x_send(n, k, src, dst, d, rows, cols):
        where = (d, rows, slice(None), cols)
        xx[n, k, d] = go(
            remote(src.at[where], dst.at[where], x_s.at[n * 4 + k * 2 + d], x_r.at[n * 4 + k * 2 + d], at(dx=1 - 2 * d))
        )

    def spread(n):
        dd[n].wait_recv()
        for d in (0, 1):
            rows, cols = HALVES[n][d]
            for r in range(rows.start, rows.stop):
                XS[d, r, :, cols] = (OWN[r, xf, :, cols] + RB[r, xf, :, cols].astype(F32)).astype(BF16)
            x_send(n, 0, XS, XR, d, rows, cols)

    def combine(n):
        r0, r1, c0, c1 = RECTS[n]
        for d in (0, 1):
            xx[n, 0, d].wait_recv()
            to = xm if d else xp1
            for h in (0, 1):
                rows, cols = HALVES[n][h]
                for r in range(rows.start, rows.stop):
                    part = OWN[r, to, :, cols] + RB[r, to, :, cols].astype(F32)
                    if h == d:
                        part = part + XR[d, r, :, cols].astype(F32)
                    YS[d, r, :, cols] = part.astype(BF16)
            x_send(n, 1, YS, YR, d, slice(r0, r1), slice(c0 * 128, c1 * 128))

    def direct(n):
        r0, r1, c0, c1 = RECTS[n]
        rows, cols = slice(r0, r1), slice(c0 * 128, c1 * 128)
        dd[n].wait_recv()
        for k, buf, land, to, dx in ((2, XS, XR, xf, 2), (0, YS, YR, xp1, 1), (1, YS, YR, xm, -1)):
            j = k % 2
            for r in range(r0, r1):
                buf[j, r, :, cols] = (OWN[r, to, :, cols] + RB[r, to, :, cols].astype(F32)).astype(BF16)
            where = (j, rows, slice(None), cols)
            m = n * 4 + k
            xx[n, 1, k] = go(remote(buf.at[where], land.at[where], x_s.at[m], x_r.at[m], at(dx=dx)))

    def finish(n):
        r0, r1, c0, c1 = RECTS[n]
        for d in (0, 1, 2):
            if (n, 1, d) in xx:
                xx[n, 1, d].wait_recv()
        for q in range(c0, c1):
            yq = lax.rem(y + OFFSET[q] + 8, 8)
            cols = slice(q * 128, (q + 1) * 128)
            for r in range(r0, r1):
                zr = lax.rem(z + OFFSET[r] + 8, 8)
                pairs = OWN[r, x, :, cols] + RB[r, x, :, cols].astype(F32)
                for d in (0, 1):
                    pairs = pairs + YR[d, r, :, cols].astype(F32)
                if n > 2:
                    pairs = pairs + XR[0, r, :, cols].astype(F32)
                v = VR[lax.rem(yq, 4), lax.div(yq, 4), zr].astype(F32)
                S[r, :, cols] = (pairs * v).astype(BF16)

    tx, td = {}, {}

    def t_sib(k, xv):
        td[k] = go(remote(T.at[:, xv, c], T.at[:, xv, c], t_s.at[12 + k], t_r.at[12 + k], at(dc=1)))

    def t_first():
        for n in range(2, 8):
            tr[n].wait_recv()
        tx[0] = go(remote(T.at[:, x, c], T.at[:, x, c], t_s.at[8], t_r.at[8], at(dx=1)))
        tx[1] = go(remote(T.at[:, x, c], T.at[:, x, c], t_s.at[9], t_r.at[9], at(dx=-1)))
        t_sib(0, x)

    def t_second():
        tx[0].wait_recv()
        tx[2] = go(remote(T.at[0:4, xm, c], T.at[0:4, xm, c], t_s.at[10], t_r.at[10], at(dx=1)))
        tx[1].wait_recv()
        tx[3] = go(remote(T.at[4:8, xp1, c], T.at[4:8, xp1, c], t_s.at[11], t_r.at[11], at(dx=-1)))
        t_sib(1, xm)
        t_sib(2, xp1)

    def t_third():
        tx[2].wait_recv()
        tx[3].wait_recv()
        t_sib(3, xf)

    for i in range(4):
        forward(2, i)
    t_first()
    for i in range(4):
        forward(3, i)
    for cp in b_own:
        cp.wait()
    compute(0)
    for i in range(4):
        forward(4, i)
        if i == 0:
            spread(0)
            t_second()
    compute(1)
    compute(2)
    combine(0)
    spread(1)
    spread(2)
    for i in range(4):
        rg[0, i // 2, 4, i].wait_recv()
    compute(3)
    for i in range(4):
        rg[1, i // 2, 4, i].wait_recv()
    v_out = []
    for d in (1, 2, 3):
        v_out.append(
            go(remote(VB.at[lax.rem(yl + d, 4)], VR.at[yl], v_s.at[d - 1], v_r.at[d - 1], yl_peer(d)))
        )
    compute(4)
    direct(3)
    direct(4)
    combine(1)
    combine(2)
    t_third()
    v_own.wait()
    for cp in v_out:
        cp.wait_recv()
    for n in range(5):
        finish(n)
    for k in range(4):
        td[k].wait_recv()

    def o_send(n, src, dst, dz):
        return go(remote(src, dst, o_s.at[n], o_r.at[n], at(dz=dz)))

    left = S[...].reshape(128, 1024)
    far, third, near = {}, {}, []
    for h in (0, 1):
        for q in (2 * h, 2 * h + 1):
            cols = slice(q * 256, (q + 1) * 256)
            part = jnp.dot(left, T[:, :, :, :, cols].reshape(1024, 256), preferred_element_type=F32)
            part = part.reshape(8, 16, 256)
            for k in range(3):
                OO[k, :, cols] = part[SLOT[(0, 2, -2)[k]]]
            OB[:, :, cols] = part.astype(BF16)
        far[h] = o_send(h, OB.at[0, :, half[h]], OH.at[h], 2 - 4 * h)
        for d in (0, 1):
            third[h, d] = o_send(2 + 2 * h + d, OB.at[SLOT[3 - 6 * d], :, half[h]], OA.at[d, :, half[h]], 1 - 2 * d)
    near = [o_send(6 + d, OB.at[SLOT[1 - 2 * d]], OR.at[d], 1 - 2 * d) for d in (0, 1)]
    for h in (0, 1):
        far[h].wait_recv()
        for d in (0, 1):
            third[h, d].wait_recv()
            joined = OO[1 + d, :, half[h]] + OA[d, :, half[h]].astype(F32)
            if h == d:
                joined = joined + OH[d].astype(F32)
            OC[d, :, half[h]] = joined.astype(BF16)
            near.append(o_send(8 + 2 * h + d, OC.at[d, :, half[h]], OR.at[2 + d, :, half[h]], 2 - 4 * d))
    for cp in near:
        cp.wait_recv()
    total = OO[0]
    for n in range(4):
        total = total + OR[n].astype(F32)
    out[...] = total
    for cp in started:
        cp.wait_send()


def body(orbitals, targets, coulomb):
    any_, dma = pl.BlockSpec(memory_space=pl.ANY), pltpu.SemaphoreType.DMA
    return pl.pallas_call(
        kernel,
        out_shape=jax.ShapeDtypeStruct((16, NB), F32),
        in_specs=[any_] * 3,
        out_specs=pl.BlockSpec(memory_space=pltpu.VMEM),
        scratch_shapes=[
            pltpu.VMEM((16, 8 * KS), BF16),
            pltpu.VMEM((8, 4, 2, 16, KS), BF16),
            pltpu.VMEM((8, 4, 2, 16, KS), BF16),
            pltpu.VMEM((8, 4, 2, 16, NB), BF16),
            pltpu.VMEM((8, 4, 16, 1024), BF16),
            pltpu.VMEM((8, 4, 16, 1024), BF16),
            pltpu.VMEM((8, 4, 16, 1024), F32),
            pltpu.VMEM((2, 8, 16, 1024), BF16),
            pltpu.VMEM((2, 8, 16, 1024), BF16),
            pltpu.VMEM((2, 8, 16, 1024), BF16),
            pltpu.VMEM((2, 8, 16, 1024), BF16),
            pltpu.VMEM((512, 256), F32),
            pltpu.VMEM((4, 2, 8, 16, 128), BF16),
            pltpu.VMEM((4, 2, 8, 16, 128), BF16),
            pltpu.VMEM((8, 16, 1024), BF16),
            pltpu.VMEM((8, 16, NB), BF16),
            pltpu.VMEM((2, 16, NB), BF16),
            pltpu.VMEM((2, 16, NB // 2), BF16),
            pltpu.VMEM((2, 16, NB), BF16),
            pltpu.VMEM((4, 16, NB), BF16),
            pltpu.VMEM((3, 16, NB), F32),
            dma((9,)),
            dma((7,)), dma((7,)),
            dma((64,)), dma((64,)),
            dma((16,)), dma((16,)),
            dma((3,)), dma((3,)),
            dma((5,)), dma((5,)),
            dma((20,)), dma((20,)),
            dma((12,)), dma((12,)),
        ],
        compiler_params=pltpu.CompilerParams(
            collective_id=0, has_side_effects=True, vmem_limit_bytes=55040 * 1024
        ),
        cost_estimate=pl.CostEstimate(flops=2_500_000_000, bytes_accessed=4_000_000, transcendentals=0),
    )(orbitals, targets, coulomb)


def solution(mesh):
    in_specs = (P(("row", "col"), None), P(("row", "col"), None), P("row", "col"))
    return jax.shard_map(
        body, mesh=mesh, in_specs=in_specs, out_specs=P(("row", "col"), None), check_vma=False
    )
```
